256 devices in a mesh: rep: 32 (over y_lo, z, core), fsdp: 8 (over y_hi, x).
Axes of the slice: x: 4, y: 4 (y_hi: 2, y_lo: 2; y = y_hi * 2 + y_lo), z: 8, core: 2. Of those that a mesh axis runs over, the one named last changes fastest.
Arguments:
- tokens: bfloat16 [65536, 5120], P(('rep', 'fsdp')), may hold values from -6 to 6
- value_cotangent: bfloat16 [65536, 512], P(('rep', 'fsdp')), may hold values from -6 to 6
- value_weight: bfloat16 [32, 5120, 512], P('rep', 'fsdp'), may hold values from -0.078125 to 0.078125
- outer_delta: float32 [32, 5120, 512], P('rep', 'fsdp'), may hold values from -3 to 3
- momentum: float32 [5120, 512], P('fsdp'), may hold values from -3 to 3
- global_weight: float32 [5120, 512], P('fsdp'), may hold values from -3 to 3
Outputs:
- values: bfloat16 [65536, 512], P(('rep', 'fsdp'))
- token_grad: bfloat16 [65536, 5120], P(('rep', 'fsdp'))
- weight_grad: bfloat16 [32, 5120, 512], P('rep', 'fsdp')
- new_momentum: float32 [5120, 512], P('fsdp')
- new_global: float32 [5120, 512], P('fsdp')
The draws below stay inside these ranges and needn't reach their ends.
All inputs are finite; a program needn't handle non-finite values.
Results may differ from the reference program's by a relative error of at most 0.007.
Values may be sent and summed in bfloat16 or wider, within the bound.
No kernel may reach another device: no remote copies, remote signals or barrier semaphores. Data moves between devices by JAX's collectives and lax.ppermute only.
A program may use at most 128 MiB of HBM per device.

```python
import jax
import jax.numpy as jnp
from jax import lax

D = 5120
KV = 512
TOK_DEV = 256
TOKENS = 65536
N_REP = 32
N_FSDP = 8


def level_of(own_key, dims, pieces, smallest, top_value):
    level, own = 1.0, jax.random.fold_in(own_key, 6)
    for dim, parts in pieces:
        draws = jnp.exp(jax.random.uniform(jax.random.fold_in(own, dim), (parts,), jnp.float32, smallest / len(pieces), top_value / len(pieces)))
        level = level * jnp.repeat(draws, dims[dim] // parts).reshape([-1 if axis == dim else 1 for axis in range(len(dims))])
    return level


def gaussian(rng, extent, deviation, bound, pieces=(), kind=jnp.bfloat16):
    entries = deviation * jax.random.normal(rng, extent, jnp.float32)
    if pieces:
        entries = entries * level_of(rng, extent, pieces, -0.22, 0.18)
    return jnp.clip(entries, -bound, bound).astype(kind)


def setup_inputs(seed: int = 0) -> dict:
    key_list = jax.random.split(jax.random.key(seed), 7)
    return {
        "tokens": gaussian(key_list[0], (TOKENS, D), 1.0, 6.0, ((0, 256),)),
        "value_cotangent": gaussian(key_list[1], (TOKENS, KV), 1.0, 6.0, ((0, 256),)),
        "value_weight": gaussian(key_list[2], (N_REP, D, KV), D ** -0.5, 0.078125, ((0, 32), (1, 8))),
        "outer_delta": gaussian(key_list[3], (N_REP, D, KV), 0.2, 3.0, ((0, 32), (1, 8)), jnp.float32),
        "momentum": gaussian(key_list[4], (D, KV), 0.2, 3.0, ((0, 8),), jnp.float32),
        "global_weight": gaussian(key_list[5], (D, KV), 0.2, 3.0, ((0, 8),), jnp.float32),
    }


def reference(tokens, value_cotangent, value_weight, outer_delta, momentum, global_weight):
    group = TOK_DEV * N_FSDP
    token_blocks = tokens.reshape(N_REP, group, D)
    cot_blocks = value_cotangent.reshape(N_REP, group, KV)

    def replica_step(items):
        x_rows, g_rows, weight = items
        values = jnp.dot(x_rows, weight, preferred_element_type=jnp.float32).astype(jnp.bfloat16)
        token_grad = lax.dot_general(g_rows, weight, (((1,), (1,)), ((), ())), preferred_element_type=jnp.float32).astype(jnp.bfloat16)
        weight_grad = lax.dot_general(x_rows, g_rows, (((0,), (0,)), ((), ())), preferred_element_type=jnp.float32).astype(jnp.bfloat16)
        return values, token_grad, weight_grad

    values, token_grad, weight_grad = lax.map(replica_step, (token_blocks, cot_blocks, value_weight))
    average = jnp.sum(outer_delta, axis=0) / jnp.float32(N_REP)
    new_momentum = 0.9 * momentum + average
    new_global = global_weight - 0.7 * (average + 0.9 * new_momentum)
    return values.reshape(TOKENS, KV), token_grad.reshape(TOKENS, D), weight_grad, new_momentum, new_global
```

```python
import itertools

import jax
import jax.numpy as jnp
from jax import lax
from jax.experimental import pallas as pl
from jax.experimental.pallas import tpu as pltpu
from jax.sharding import PartitionSpec as P

AXES = ("rep", "fsdp")
GRID = (2, 8, 2, 2, 4)
F32, BF16 = jnp.float32, jnp.bfloat16


def flat(place):
    index = 0
    for coordinate, size in zip(place, GRID):
        index = index * size + coordinate % size
    return index


def permutation(move):
    return [(flat(c), flat(move(*c))) for c in itertools.product(*map(range, GRID))]


def along_x(step):
    return permutation(lambda l, z, c, h, x: (l, z, c, h, x + step))


def along_z(step):
    return permutation(lambda l, z, c, h, x: (l, z + step, c, h, x))


def flip(dl, dz, dc, dh):
    return permutation(lambda l, z, c, h, x: (l ^ dl, z ^ dz, c ^ dc, h ^ dh, x))


def send(value, moves):
    return lax.ppermute(value, AXES, moves)


def dot_t(a, b):
    return lax.dot_general(a, b, (((0,), (0,)), ((), ())), preferred_element_type=F32)


def whole(shape):
    return pl.BlockSpec(shape, lambda i, s: (0,) * len(shape))


def call(kernel, scalars, operands, specs, outs, out_specs, flops, moved, aliases={}):
    return pl.pallas_call(
        kernel,
        grid_spec=pltpu.PrefetchScalarGridSpec(
            num_scalar_prefetch=1, grid=(1,), in_specs=specs, out_specs=out_specs
        ),
        out_shape=outs,
        input_output_aliases=aliases,
        cost_estimate=pl.CostEstimate(flops=flops, bytes_accessed=moved, transcendentals=0),
        compiler_params=pltpu.CompilerParams(vmem_limit_bytes=40 * 2**20),
    )(scalars, *operands)


def local(tokens, value_cotangent, value_weight, outer_delta, momentum, global_weight):
    rep, fsdp = lax.axis_index("rep"), lax.axis_index("fsdp")
    y_lo, z, core = rep // 16, (rep // 2) % 8, rep % 2
    y_hi, x = fsdp // 4, fsdp % 4
    rows, feats = value_weight.shape[1:]
    toks = tokens.shape[0]
    half = rows // 2
    weight = value_weight[0]

    def ring(own):
        left = send(own, along_x(1))
        right = send(own, along_x(-1))
        return left, right

    def ring_on(left, right):
        top = send(left[:half], along_x(1))
        bottom = send(right[half:], along_x(-1))
        return top, bottom

    def column(plane, r):
        return plane * 4 + (x + r) % 4

    def block_for_partner(r):
        return lax.dynamic_slice(
            tokens, (0, column(1 - y_hi, r) * rows), (toks, rows)
        )

    across = flip(0, 0, 0, 1)
    left0, right0 = ring(weight)
    got = send(jnp.concatenate([value_cotangent, block_for_partner(2)], axis=1), across)
    g_other, x_other2 = got[:, :feats], got[:, feats:]
    weight1 = send(weight, across)
    got = send(
        jnp.concatenate([block_for_partner(1), block_for_partner(3), block_for_partner(0)], axis=1),
        across,
    )
    x_other130 = got

    top0, bottom0 = ring_on(left0, right0)

    scal_w = jnp.stack([column(y_hi, r) for r in range(4)]).astype(jnp.int32)

    def first_kernel(s, xa, ga, xb, gb, up, down):
        part = dot_t(xa[...], ga[...]) + dot_t(xb[...], gb[...])
        up[...] = part[:half].astype(BF16)
        down[...] = part[half:].astype(BF16)

    half_out = jax.ShapeDtypeStruct((half, feats), BF16)
    up, down = call(
        first_kernel,
        scal_w,
        (tokens, value_cotangent, x_other2, g_other),
        [pl.BlockSpec((toks, rows), lambda i, s: (0, s[2])), whole((toks, feats)), whole((toks, rows)), whole((toks, feats))],
        (half_out, half_out),
        (whole((half, feats)), whole((half, feats))),
        4 * toks * rows * feats,
        2 * toks * (2 * rows + 2 * feats) + 2 * rows * feats,
    )
    from_left = send(up, along_x(1))
    from_right = send(down, along_x(-1))

    left1, right1 = ring(weight1)
    top1, bottom1 = ring_on(left1, right1)

    def second_kernel(s, xa1, xa3, xa0, ga, xb, gb, ina, inb, out1, out3, out0):
        g0, g1 = ga[...], gb[...]
        part = dot_t(xa1[...], g0) + dot_t(xb[:, :rows], g1)
        out1[:half] = (part[:half] + ina[...].astype(F32)).astype(BF16)
        out1[half:] = part[half:].astype(BF16)
        part = dot_t(xa3[...], g0) + dot_t(xb[:, rows : 2 * rows], g1)
        out3[:half] = part[:half].astype(BF16)
        out3[half:] = (part[half:] + inb[...].astype(F32)).astype(BF16)
        out0[...] = dot_t(xa0[...], g0) + dot_t(xb[:, 2 * rows :], g1)

    full_out = jax.ShapeDtypeStruct((rows, feats), BF16)
    out1, out3, part0 = call(
        second_kernel,
        scal_w,
        (tokens, tokens, tokens, value_cotangent, x_other130, g_other, from_left, from_right),
        [
            pl.BlockSpec((toks, rows), lambda i, s: (0, s[1])),
            pl.BlockSpec((toks, rows), lambda i, s: (0, s[3])),
            pl.BlockSpec((toks, rows), lambda i, s: (0, s[0])),
            whole((toks, feats)),
            whole((toks, 3 * rows)),
            whole((toks, feats)),
            whole((half, feats)),
            whole((half, feats)),
        ],
        (full_out, full_out, jax.ShapeDtypeStruct((rows, feats), F32)),
        (whole((rows, feats)),) * 3,
        12 * toks * rows * feats,
        2 * toks * (6 * rows + 2 * feats) + 10 * rows * feats,
    )
    sum_left = send(out1, along_x(1))
    sum_right = send(out3, along_x(-1))
    weight_grad = (part0 + sum_left.astype(F32) + sum_right.astype(F32)).astype(BF16)[None]

    def forward(plane, own, left, right, top, bottom, grad_so_far, values_so_far):
        last = values_so_far is not None

        def kernel(s, xr, g, w0, w3, w1, w2a, w2b, *rest):
            if last:
                _, before, grad, vals = rest
            else:
                grad, vals = rest
            total = before[...] if last else jnp.zeros((toks, feats), F32)
            cot = g[...]
            pieces = ((w0, 0, 0), (w3, 3, 0), (w1, 1, 0), (w2a, 2, 0), (w2b, 2, half))
            for ref, r, shift in pieces:
                w = ref[...]
                at = pl.multiple_of(s[1 + r] * rows, 128)
                if shift == 0 and w.shape[0] == rows:
                    total += jnp.dot(xr[:, pl.ds(at, rows)], w, preferred_element_type=F32)
                    grad[:, pl.ds(at, rows)] = lax.dot_general(
                        cot, w, (((1,), (1,)), ((), ())), preferred_element_type=F32
                    ).astype(BF16)
            w = jnp.concatenate([w2a[...], w2b[...]], axis=0)
            at = pl.multiple_of(s[3] * rows, 128)
            total += jnp.dot(xr[:, pl.ds(at, rows)], w, preferred_element_type=F32)
            grad[:, pl.ds(at, rows)] = lax.dot_general(
                cot, w, (((1,), (1,)), ((), ())), preferred_element_type=F32
            ).astype(BF16)
            vals[...] = total.astype(vals.dtype)

        scalars = jnp.stack([plane] + [(x + r) % 4 for r in range(4)]).astype(jnp.int32)
        plane_spec = pl.BlockSpec((toks, 4 * rows), lambda i, s: (0, s[0]))
        operands = [tokens, value_cotangent, own, left, right, top, bottom]
        specs = [plane_spec, whole((toks, feats))] + [whole((rows, feats))] * 3 + [whole((half, feats))] * 2
        aliases = {}
        if last:
            operands += [grad_so_far, values_so_far]
            specs += [pl.BlockSpec(memory_space=pl.ANY), whole((toks, feats))]
            aliases = {8: 0}
        return call(
            kernel,
            scalars,
            operands,
            specs,
            (jax.ShapeDtypeStruct(tokens.shape, BF16), jax.ShapeDtypeStruct((toks, feats), BF16 if last else F32)),
            (plane_spec, whole((toks, feats))),
            16 * toks * rows * feats,
            2 * (8 * toks * rows + 4 * rows * feats + 4 * toks * feats),
            aliases,
        )

    grad, partial_values = forward(y_hi, weight, left0, right0, top0, bottom0, None, None)
    token_grad, values = forward(1 - y_hi, weight1, left1, right1, top1, bottom1, grad, partial_values)

    delta = outer_delta[0]
    quarter = rows // 4
    eighth = rows // 8
    q = y_lo * 2 + core

    def quarter_of(r):
        return lax.dynamic_slice(delta, ((q ^ r) * quarter, 0), (quarter, feats))

    moves = {1: flip(0, 0, 1, 0), 2: flip(1, 0, 0, 0), 3: flip(1, 0, 1, 0)}
    total = quarter_of(0)
    for r in (1, 2, 3):
        total = total + send(quarter_of(r).astype(BF16), moves[r]).astype(F32)
    par = z % 2
    keep = lax.dynamic_slice(total, (par * eighth, 0), (eighth, feats))
    give = lax.dynamic_slice(total, ((1 - par) * eighth, 0), (eighth, feats))
    pair = flip(0, 1, 0, 0)
    total = (keep + send(give.astype(BF16), pair).astype(F32)).astype(BF16)
    up2, down2, far = send(total, along_z(2)), send(total, along_z(-2)), send(total, along_z(4))
    total = ((total.astype(F32) + far.astype(F32)) + (up2.astype(F32) + down2.astype(F32))).astype(BF16)
    other = send(total, pair)
    total = lax.select(
        par == 0, jnp.concatenate([total, other], axis=0), jnp.concatenate([other, total], axis=0)
    )
    parts = [total] + [send(total, moves[r]) for r in (1, 2, 3)]

    def update_kernel(s, a, b, c, d, mom, glob, new_mom, new_glob):
        for r, ref in enumerate((a, b, c, d)):
            here = pl.ds(pl.multiple_of((s[0] ^ r) * quarter, 16), quarter)
            average = ref[...].astype(F32) / jnp.float32(32)
            moment = 0.9 * mom[here] + average
            new_mom[here] = moment
            new_glob[here] = glob[here] - 0.7 * (average + 0.9 * moment)

    state = jax.ShapeDtypeStruct((rows, feats), F32)
    new_momentum, new_global = call(
        update_kernel,
        q.astype(jnp.int32)[None],
        (*parts, momentum, global_weight),
        [whole((quarter, feats))] * 4 + [whole((rows, feats))] * 2,
        (state, state),
        (whole((rows, feats)),) * 2,
        8 * rows * feats,
        18 * rows * feats,
    )
    return (values, token_grad, weight_grad, new_momentum, new_global)


def solution(mesh):
    in_specs = (
        P(("rep", "fsdp"), None),
        P(("rep", "fsdp"), None),
        P("rep", "fsdp", None),
        P("rep", "fsdp", None),
        P("fsdp", None),
        P("fsdp", None),
    )
    out_specs = (
        P(("rep", "fsdp"), None),
        P(("rep", "fsdp"), None),
        P("rep", "fsdp", None),
        P("fsdp", None),
        P("fsdp", None),
    )
    return jax.shard_map(local, mesh=mesh, in_specs=in_specs, out_specs=out_specs, check_vma=False)
```

```python
import itertools

import jax
import jax.numpy as jnp
from jax import lax
from jax.experimental import pallas as pl
from jax.experimental.pallas import tpu as pltpu
from jax.sharding import PartitionSpec as P

AXES = ("rep", "fsdp")
GRID = (2, 8, 2, 2, 4)
F32, BF16 = jnp.float32, jnp.bfloat16


def flat(place):
    index = 0
    for coordinate, size in zip(place, GRID):
        index = index * size + coordinate % size
    return index


def permutation(move):
    return [(flat(c), flat(move(*c))) for c in itertools.product(*map(range, GRID))]


def along_x(step):
    return permutation(lambda l, z, c, h, x: (l, z, c, h, x + step))


def along_z(step):
    return permutation(lambda l, z, c, h, x: (l, z + step, c, h, x))


def flip(dl, dz, dc, dh):
    return permutation(lambda l, z, c, h, x: (l ^ dl, z ^ dz, c ^ dc, h ^ dh, x))


def send(value, moves):
    return lax.ppermute(value, AXES, moves)


def after(value, *others):
    return lax.optimization_barrier((value, *others))[0]


def dot_t(a, b):
    return lax.dot_general(a, b, (((0,), (0,)), ((), ())), preferred_element_type=F32)


def whole(shape):
    return pl.BlockSpec(shape, lambda i, s: (0,) * len(shape))


def call(kernel, scalars, operands, specs, outs, out_specs, flops, moved, aliases={}, scratch=()):
    return pl.pallas_call(
        kernel,
        grid_spec=pltpu.PrefetchScalarGridSpec(
            num_scalar_prefetch=1, grid=(1,), in_specs=specs, out_specs=out_specs, scratch_shapes=scratch
        ),
        out_shape=outs,
        input_output_aliases=aliases,
        cost_estimate=pl.CostEstimate(flops=flops, bytes_accessed=moved, transcendentals=0),
        compiler_params=pltpu.CompilerParams(vmem_limit_bytes=32 * 2**20),
    )(scalars, *operands)


def local(tokens, value_cotangent, value_weight, outer_delta, momentum, global_weight):
    rep, fsdp = lax.axis_index("rep"), lax.axis_index("fsdp")
    y_lo, z, core = rep // 16, (rep // 2) % 8, rep % 2
    y_hi, x = fsdp // 4, fsdp % 4
    rows, feats = value_weight.shape[1:]
    toks = tokens.shape[0]
    half = rows // 2
    weight = value_weight[0]

    def ring(own):
        return send(own, right_on), send(own, left_on)


    def column(plane, r):
        return plane * 4 + (x + r) % 4

    def block_for_partner(r):
        return lax.dynamic_slice(tokens, (0, column(1 - y_hi, r) * rows), (toks, rows))

    across = flip(0, 0, 0, 1)
    right_on, left_on = along_x(1), along_x(-1)

    left0, right0 = send(weight, right_on), send(weight, left_on)
    weight1 = send(weight, across)

    delta = outer_delta[0]
    halves, quarter = rows // 2, rows // 4
    pair_c, pair_l, pair_z = flip(0, 0, 1, 0), flip(1, 0, 0, 0), flip(0, 1, 0, 0)
    mine = lax.dynamic_slice(delta, (core * halves, 0), (halves, feats))
    give = lax.dynamic_slice(delta, ((1 - core) * halves, 0), (halves, feats)).astype(BF16)
    total = mine + send(give, pair_c).astype(F32)
    bit = z % 2
    give = lax.dynamic_slice(total, ((1 - bit) * quarter, 0), (quarter, feats)).astype(BF16)
    total = lax.dynamic_slice(total, (bit * quarter, 0), (quarter, feats))
    total = (total + send(give, pair_z).astype(F32)).astype(BF16)

    def pack_kernel(s, x2, x1, x3, x0, cot, one, two):
        one[:, :rows] = x2[...]
        one[:, rows:] = cot[...]
        two[:, :rows] = x1[...]
        two[:, rows : 2 * rows] = x3[...]
        two[:, 2 * rows :] = x0[...]

    def block_of(k):
        return pl.BlockSpec((toks, rows), lambda i, s: (0, s[k]))

    first, rest = call(
        pack_kernel,
        jnp.stack([column(1 - y_hi, r) for r in range(4)]).astype(jnp.int32),
        (tokens, tokens, tokens, tokens, value_cotangent),
        [block_of(2), block_of(1), block_of(3), block_of(0), whole((toks, feats))],
        (
            jax.ShapeDtypeStruct((toks, rows + feats), BF16),
            jax.ShapeDtypeStruct((toks, 3 * rows), BF16),
        ),
        (whole((toks, rows + feats)), whole((toks, 3 * rows))),
        0,
        4 * toks * (4 * rows + feats),
    )
    first = send(first, across)
    rest = send(after(rest, weight1, left0, right0), across)

    left1, right1 = ring(after(weight1, left0, right0))

    total = after(total, left0, right0, weight1)
    for step in (2, 6):
        got = send(total, flip(0, step, 0, 0))
        total = (total.astype(F32) + got.astype(F32)).astype(BF16)

    def forward(pieces, specs_of):
        n = len(pieces)
        count = sum(len(k) for _, _, k in pieces)

        def kernel(s, g, *refs):
            xs, weights = refs[:n], refs[n : n + count]
            grad, vals, block, sems = refs[-4:]
            total = jnp.zeros((toks, feats), F32)
            cot = g[...]
            at_ref = 0
            copies = []
            for i, (_, _, kinds) in enumerate(pieces):
                w = [ref[...] for ref in weights[at_ref : at_ref + len(kinds)]]
                at_ref += len(kinds)
                w = w[0] if len(w) == 1 else jnp.concatenate(w, axis=0)
                block[i] = lax.dot_general(
                    cot, w, (((1,), (1,)), ((), ())), preferred_element_type=F32
                ).astype(BF16)
                here = pl.ds(pl.multiple_of(s[i] * rows, 128), rows)
                copies.append(pltpu.make_async_copy(block.at[i], grad.at[:, here], sems.at[i]))
                copies[-1].start()
                total += jnp.dot(xs[i][...], w, preferred_element_type=F32)
            vals[...] = total.astype(vals.dtype)
            for copy in copies:
                copy.wait()

        scalars = jnp.stack([column(plane, r) for plane, r, _ in pieces]).astype(jnp.int32)
        operands = [value_cotangent] + [tokens] * n + [k for _, _, kinds in pieces for k in kinds]
        specs = [whole((toks, feats))]
        specs += [pl.BlockSpec((toks, rows), lambda i, s, j=j: (0, s[j])) for j in range(n)]
        specs += specs_of
        return call(
            kernel,
            scalars,
            operands,
            specs,
            (jax.ShapeDtypeStruct(tokens.shape, BF16), jax.ShapeDtypeStruct((toks, feats), F32)),
            (pl.BlockSpec(memory_space=pl.ANY), whole((toks, feats))),
            4 * n * toks * rows * feats,
            2 * n * (2 * toks * rows + rows * feats) + 8 * toks * feats,
            {},
            [pltpu.VMEM((n, toks, rows), BF16), pltpu.SemaphoreType.DMA((n,))],
        )

    blocks = [whole((rows, feats))] * 4
    scal_w = jnp.stack([column(y_hi, r) for r in range(4)]).astype(jnp.int32)
    part = whole((half, feats))

    def block_of_own(k):
        return pl.BlockSpec((toks, rows), lambda i, s: (0, s[k]))

    def first_kernel(s, xa, ga, xg, left, right, up, down):
        total = dot_t(xa[...], ga[...]) + dot_t(xg[:, :rows], xg[:, rows:])
        up[:half] = left[...]
        down[:half] = right[...]
        up[half:] = total[:half].astype(BF16)
        down[half:] = total[half:].astype(BF16)

    up, down = call(
        first_kernel,
        scal_w,
        (tokens, value_cotangent, first, left0, right0),
        [
            block_of_own(2),
            whole((toks, feats)),
            whole((toks, rows + feats)),
            part,
            pl.BlockSpec((half, feats), lambda i, s: (1, 0)),
        ],
        (jax.ShapeDtypeStruct((rows, feats), BF16),) * 2,
        (whole((rows, feats)),) * 2,
        4 * toks * rows * feats,
        2 * toks * (2 * rows + 2 * feats) + 2 * rows * feats,
    )
    up, down, _, _ = lax.optimization_barrier((up, down, left1, right1))
    from_left, from_right = send(up, right_on), send(down, left_on)


    def second_kernel(s, xa1, xa3, xa0, ga, xb, xg, one, three, own):
        g0, g1 = ga[...], xg[:, rows:]
        one[...] = dot_t(xa1[...], g0) + dot_t(xb[:, :rows], g1)
        three[...] = dot_t(xa3[...], g0) + dot_t(xb[:, rows : 2 * rows], g1)
        own[...] = dot_t(xa0[...], g0) + dot_t(xb[:, 2 * rows :], g1)

    one, three, own = call(
        second_kernel,
        scal_w,
        (tokens, tokens, tokens, value_cotangent, rest, first),
        [
            block_of_own(1),
            block_of_own(3),
            block_of_own(0),
            whole((toks, feats)),
            whole((toks, 3 * rows)),
            whole((toks, rows + feats)),
        ],
        (jax.ShapeDtypeStruct((rows, feats), F32),) * 3,
        (whole((rows, feats)),) * 3,
        12 * toks * rows * feats,
        2 * toks * (6 * rows + 2 * feats) + 10 * rows * feats,
    )

    def third_kernel(s, one, three, left, right, up, down, far):
        far[:half] = left[:half]
        far[half:] = right[:half]
        up[:half] = (one[:half] + left[half:].astype(F32)).astype(BF16)
        up[half:] = one[half:].astype(BF16)
        down[:half] = three[:half].astype(BF16)
        down[half:] = (three[half:] + right[half:].astype(F32)).astype(BF16)

    up, down, far1 = call(
        third_kernel,
        scal_w,
        (one, three, from_left, from_right),
        [whole((rows, feats))] * 4,
        (jax.ShapeDtypeStruct((rows, feats), BF16),) * 3,
        (whole((rows, feats)),) * 3,
        2 * rows * feats,
        14 * rows * feats,
    )
    sum_left, sum_right = send(up, right_on), send(down, left_on)
    far1 = send(far1, across)

    total = after(total, rest)
    got = send(total, pair_l)
    total = (total.astype(F32) + got.astype(F32)).astype(BF16)
    got = send(total, pair_z)
    total = lax.select(bit == 0, jnp.concatenate([total, got]), jnp.concatenate([got, total]))
    got = send(total, pair_c)

    def update_kernel(s, a, b, mom, glob, new_mom, new_glob):
        for r, ref in enumerate((a, b)):
            here = pl.ds(pl.multiple_of((s[0] ^ r) * halves, 16), halves)
            average = ref[...].astype(F32) / jnp.float32(32)
            moment = 0.9 * mom[here] + average
            new_mom[here] = moment
            new_glob[here] = glob[here] - 0.7 * (average + 0.9 * moment)

    state = jax.ShapeDtypeStruct((rows, feats), F32)
    new_momentum, new_global = call(
        update_kernel,
        core.astype(jnp.int32)[None],
        (total, got, momentum, global_weight),
        [whole((halves, feats))] * 2 + [whole((rows, feats))] * 2,
        (state, state),
        (whole((rows, feats)),) * 2,
        8 * rows * feats,
        18 * rows * feats,
    )

    full = whole((rows, feats))
    grad, partial_values = forward(
        [
            (1 - y_hi, 0, (weight1,)),
            (1 - y_hi, 3, (left1,)),
            (1 - y_hi, 1, (right1,)),
            (y_hi, 0, (weight,)),
            (y_hi, 3, (left0,)),
            (y_hi, 1, (right0,)),
            (y_hi, 2, (from_left, from_right)),
        ],
        [full] * 6 + [part] * 2,
    )

    def last_kernel(s, g, xr, w, before, own, a, b, old, grad, vals, out):
        w = w[...]
        grad[...] = lax.dot_general(
            g[...], w, (((1,), (1,)), ((), ())), preferred_element_type=F32
        ).astype(BF16)
        vals[...] = (before[...] + jnp.dot(xr[...], w, preferred_element_type=F32)).astype(BF16)
        out[0] = (own[...] + a[...].astype(F32) + b[...].astype(F32)).astype(BF16)

    last_block = pl.BlockSpec((toks, rows), lambda i, s: (0, s[0]))
    token_grad, values, weight_grad = call(
        last_kernel,
        column(1 - y_hi, 2).astype(jnp.int32)[None],
        (value_cotangent, tokens, far1, partial_values, own, sum_left, sum_right, grad),
        [whole((toks, feats)), last_block, full, whole((toks, feats))] + [full] * 3 + [pl.BlockSpec(memory_space=pl.ANY)],
        (
            jax.ShapeDtypeStruct(tokens.shape, BF16),
            jax.ShapeDtypeStruct((toks, feats), BF16),
            jax.ShapeDtypeStruct((1, rows, feats), BF16),
        ),
        (last_block, whole((toks, feats)), whole((1, rows, feats))),
        4 * toks * rows * feats,
        2 * (2 * toks * rows + rows * feats) + 8 * toks * feats + 10 * rows * feats,
        {8: 0},
    )
    return (values, token_grad, weight_grad, new_momentum, new_global)


def solution(mesh):
    in_specs = (
        P(("rep", "fsdp"), None),
        P(("rep", "fsdp"), None),
        P("rep", "fsdp", None),
        P("rep", "fsdp", None),
        P("fsdp", None),
        P("fsdp", None),
    )
    out_specs = (
        P(("rep", "fsdp"), None),
        P(("rep", "fsdp"), None),
        P("rep", "fsdp", None),
        P("fsdp", None),
        P("fsdp", None),
    )
    return jax.shard_map(local, mesh=mesh, in_specs=in_specs, out_specs=out_specs, check_vma=False)
```

```python
import itertools

import jax
import jax.numpy as jnp
from jax import lax
from jax.experimental import pallas as pl
from jax.experimental.pallas import tpu as pltpu
from jax.sharding import PartitionSpec as P

AXES = ("rep", "fsdp")
GRID = (2, 8, 2, 2, 4)
F32, BF16 = jnp.float32, jnp.bfloat16


def flat(place):
    index = 0
    for coordinate, size in zip(place, GRID):
        index = index * size + coordinate % size
    return index


def permutation(move):
    return [(flat(c), flat(move(*c))) for c in itertools.product(*map(range, GRID))]


def along_x(step):
    return permutation(lambda l, z, c, h, x: (l, z, c, h, x + step))


def along_z(step):
    return permutation(lambda l, z, c, h, x: (l, z + step, c, h, x))


def flip(dl, dz, dc, dh):
    return permutation(lambda l, z, c, h, x: (l ^ dl, z ^ dz, c ^ dc, h ^ dh, x))


def send(value, moves):
    return lax.ppermute(value, AXES, moves)


def after(value, *others):
    return lax.optimization_barrier((value, *others))[0]


def dot_t(a, b):
    return lax.dot_general(a, b, (((0,), (0,)), ((), ())), preferred_element_type=F32)


def whole(shape):
    return pl.BlockSpec(shape, lambda i, s: (0,) * len(shape))


def call(kernel, scalars, operands, specs, outs, out_specs, flops, moved, aliases={}, scratch=(), vmem=32):
    return pl.pallas_call(
        kernel,
        grid_spec=pltpu.PrefetchScalarGridSpec(
            num_scalar_prefetch=1, grid=(1,), in_specs=specs, out_specs=out_specs, scratch_shapes=scratch
        ),
        out_shape=outs,
        input_output_aliases=aliases,
        cost_estimate=pl.CostEstimate(flops=flops, bytes_accessed=moved, transcendentals=0),
        compiler_params=pltpu.CompilerParams(vmem_limit_bytes=vmem * 2**20),
    )(scalars, *operands)


def local(tokens, value_cotangent, value_weight, outer_delta, momentum, global_weight):
    rep, fsdp = lax.axis_index("rep"), lax.axis_index("fsdp")
    y_lo, z, core = rep // 16, (rep // 2) % 8, rep % 2
    y_hi, x = fsdp // 4, fsdp % 4
    rows, feats = value_weight.shape[1:]
    toks = tokens.shape[0]
    half = rows // 2
    weight = value_weight[0]

    def ring(own):
        return send(own, right_on), send(own, left_on)


    def column(plane, r):
        return plane * 4 + (x + r) % 4

    def block_for_partner(r):
        return lax.dynamic_slice(tokens, (0, column(1 - y_hi, r) * rows), (toks, rows))

    across = flip(0, 0, 0, 1)
    right_on, left_on = along_x(1), along_x(-1)

    left0, right0 = send(weight, right_on), send(weight, left_on)
    weight1 = send(weight, across)

    delta = outer_delta[0]
    halves, quarter = rows // 2, rows // 4
    pair_c, pair_l, pair_z = flip(0, 0, 1, 0), flip(1, 0, 0, 0), flip(0, 1, 0, 0)
    mine = lax.dynamic_slice(delta, (core * halves, 0), (halves, feats))
    give = lax.dynamic_slice(delta, ((1 - core) * halves, 0), (halves, feats)).astype(BF16)
    total = mine + send(give, pair_c).astype(F32)
    bit = z % 2
    give = lax.dynamic_slice(total, ((1 - bit) * quarter, 0), (quarter, feats)).astype(BF16)
    total = lax.dynamic_slice(total, (bit * quarter, 0), (quarter, feats))
    total = (total + send(give, pair_z).astype(F32)).astype(BF16)

    def pack_kernel(s, x2, x1, x3, x0, cot, one, two):
        one[:, :rows] = x2[...]
        one[:, rows:] = cot[...]
        two[:, :rows] = x1[...]
        two[:, rows : 2 * rows] = x3[...]
        two[:, 2 * rows :] = x0[...]

    def block_of(k):
        return pl.BlockSpec((toks, rows), lambda i, s: (0, s[k]))

    first, rest = call(
        pack_kernel,
        jnp.stack([column(1 - y_hi, r) for r in range(4)]).astype(jnp.int32),
        (tokens, tokens, tokens, tokens, value_cotangent),
        [block_of(2), block_of(1), block_of(3), block_of(0), whole((toks, feats))],
        (
            jax.ShapeDtypeStruct((toks, rows + feats), BF16),
            jax.ShapeDtypeStruct((toks, 3 * rows), BF16),
        ),
        (whole((toks, rows + feats)), whole((toks, 3 * rows))),
        0,
        4 * toks * (4 * rows + feats),
    )
    first = send(first, across)
    rest = send(after(rest, weight1, left0, right0), across)

    left1, right1 = ring(after(weight1, left0, right0))

    total = after(total, left0, right0, weight1)
    for step in (2, 6):
        got = send(total, flip(0, step, 0, 0))
        total = (total.astype(F32) + got.astype(F32)).astype(BF16)

    def forward(pieces, specs_of):
        n = len(pieces)
        count = sum(len(k) for _, _, k in pieces)

        def kernel(s, g, *refs):
            xs, weights = refs[:n], refs[n : n + count]
            grad, vals, block, sems = refs[-4:]
            total = jnp.zeros((toks, feats), F32)
            cot = g[...]
            at_ref = 0
            copies = []
            for i, (_, _, kinds) in enumerate(pieces):
                w = [ref[...] for ref in weights[at_ref : at_ref + len(kinds)]]
                at_ref += len(kinds)
                w = w[0] if len(w) == 1 else jnp.concatenate(w, axis=0)
                block[i] = lax.dot_general(
                    cot, w, (((1,), (1,)), ((), ())), preferred_element_type=F32
                ).astype(BF16)
                here = pl.ds(pl.multiple_of(s[i] * rows, 128), rows)
                copies.append(pltpu.make_async_copy(block.at[i], grad.at[:, here], sems.at[i]))
                copies[-1].start()
                total += jnp.dot(xs[i][...], w, preferred_element_type=F32)
            vals[...] = total.astype(vals.dtype)
            for copy in copies:
                copy.wait()

        scalars = jnp.stack([column(plane, r) for plane, r, _ in pieces]).astype(jnp.int32)
        operands = [value_cotangent] + [tokens] * n + [k for _, _, kinds in pieces for k in kinds]
        specs = [whole((toks, feats))]
        specs += [pl.BlockSpec((toks, rows), lambda i, s, j=j: (0, s[j])) for j in range(n)]
        specs += specs_of
        return call(
            kernel,
            scalars,
            operands,
            specs,
            (jax.ShapeDtypeStruct(tokens.shape, BF16), jax.ShapeDtypeStruct((toks, feats), F32)),
            (pl.BlockSpec(memory_space=pl.ANY), whole((toks, feats))),
            4 * n * toks * rows * feats,
            2 * n * (2 * toks * rows + rows * feats) + 8 * toks * feats,
            {},
            vmem=60,
            scratch=[pltpu.VMEM((n, toks, rows), BF16), pltpu.SemaphoreType.DMA((n,))],
        )

    blocks = [whole((rows, feats))] * 4
    scal_w = jnp.stack([column(y_hi, r) for r in range(4)]).astype(jnp.int32)
    part = whole((half, feats))

    def block_of_own(k):
        return pl.BlockSpec((toks, rows), lambda i, s: (0, s[k]))

    def first_kernel(s, xa, ga, xg, left, right, up, down):
        total = dot_t(xa[...], ga[...]) + dot_t(xg[:, :rows], xg[:, rows:])
        up[:half] = left[...]
        down[:half] = right[...]
        up[half:] = total[:half].astype(BF16)
        down[half:] = total[half:].astype(BF16)

    up, down = call(
        first_kernel,
        scal_w,
        (tokens, value_cotangent, first, left0, right0),
        [
            block_of_own(2),
            whole((toks, feats)),
            whole((toks, rows + feats)),
            part,
            pl.BlockSpec((half, feats), lambda i, s: (1, 0)),
        ],
        (jax.ShapeDtypeStruct((rows, feats), BF16),) * 2,
        (whole((rows, feats)),) * 2,
        4 * toks * rows * feats,
        2 * toks * (2 * rows + 2 * feats) + 2 * rows * feats,
    )
    up, down, _, _ = lax.optimization_barrier((up, down, left1, right1))
    from_left, from_right = send(up, right_on), send(down, left_on)


    def second_kernel(s, xa1, xa3, xa0, ga, xb, xg, one, three, own):
        g0, g1 = ga[...], xg[:, rows:]
        one[...] = dot_t(xa1[...], g0) + dot_t(xb[:, :rows], g1)
        three[...] = dot_t(xa3[...], g0) + dot_t(xb[:, rows : 2 * rows], g1)
        own[...] = dot_t(xa0[...], g0) + dot_t(xb[:, 2 * rows :], g1)

    one, three, own = call(
        second_kernel,
        scal_w,
        (tokens, tokens, tokens, value_cotangent, rest, first),
        [
            block_of_own(1),
            block_of_own(3),
            block_of_own(0),
            whole((toks, feats)),
            whole((toks, 3 * rows)),
            whole((toks, rows + feats)),
        ],
        (jax.ShapeDtypeStruct((rows, feats), F32),) * 3,
        (whole((rows, feats)),) * 3,
        12 * toks * rows * feats,
        2 * toks * (6 * rows + 2 * feats) + 10 * rows * feats,
    )

    def third_kernel(s, one, three, left, right, up, down, far):
        far[:half] = left[:half]
        far[half:] = right[:half]
        up[:half] = (one[:half] + left[half:].astype(F32)).astype(BF16)
        up[half:] = one[half:].astype(BF16)
        down[:half] = three[:half].astype(BF16)
        down[half:] = (three[half:] + right[half:].astype(F32)).astype(BF16)

    up, down, far1 = call(
        third_kernel,
        scal_w,
        (one, three, from_left, from_right),
        [whole((rows, feats))] * 4,
        (jax.ShapeDtypeStruct((rows, feats), BF16),) * 3,
        (whole((rows, feats)),) * 3,
        2 * rows * feats,
        14 * rows * feats,
    )
    sum_left, sum_right = send(up, right_on), send(down, left_on)
    far1 = send(far1, across)

    total = after(total, rest)
    got = send(total, pair_l)
    total = (total.astype(F32) + got.astype(F32)).astype(BF16)
    got = send(total, pair_z)
    total = lax.select(bit == 0, jnp.concatenate([total, got]), jnp.concatenate([got, total]))
    got = send(total, pair_c)

    def update_kernel(s, a, b, mom, glob, new_mom, new_glob):
        for r, ref in enumerate((a, b)):
            here = pl.ds(pl.multiple_of((s[0] ^ r) * halves, 16), halves)
            average = ref[...].astype(F32) / jnp.float32(32)
            moment = 0.9 * mom[here] + average
            new_mom[here] = moment
            new_glob[here] = glob[here] - 0.7 * (average + 0.9 * moment)

    state = jax.ShapeDtypeStruct((rows, feats), F32)
    new_momentum, new_global = call(
        update_kernel,
        core.astype(jnp.int32)[None],
        (total, got, momentum, global_weight),
        [whole((halves, feats))] * 2 + [whole((rows, feats))] * 2,
        (state, state),
        (whole((rows, feats)),) * 2,
        8 * rows * feats,
        18 * rows * feats,
    )

    full = whole((rows, feats))
    grad, partial_values = forward(
        [
            (1 - y_hi, 0, (weight1,)),
            (1 - y_hi, 3, (left1,)),
            (1 - y_hi, 1, (right1,)),
            (y_hi, 0, (weight,)),
            (y_hi, 3, (left0,)),
            (y_hi, 1, (right0,)),
            (y_hi, 2, (from_left, from_right)),
        ],
        [full] * 6 + [part] * 2,
    )

    def last_kernel(s, g, xr, w, before, own, a, b, old, grad, vals, out):
        w = w[...]
        grad[...] = lax.dot_general(
            g[...], w, (((1,), (1,)), ((), ())), preferred_element_type=F32
        ).astype(BF16)
        vals[...] = (before[...] + jnp.dot(xr[...], w, preferred_element_type=F32)).astype(BF16)
        out[0] = (own[...] + a[...].astype(F32) + b[...].astype(F32)).astype(BF16)

    last_block = pl.BlockSpec((toks, rows), lambda i, s: (0, s[0]))
    token_grad, values, weight_grad = call(
        last_kernel,
        column(1 - y_hi, 2).astype(jnp.int32)[None],
        (value_cotangent, tokens, far1, partial_values, own, sum_left, sum_right, grad),
        [whole((toks, feats)), last_block, full, whole((toks, feats))] + [full] * 3 + [pl.BlockSpec(memory_space=pl.ANY)],
        (
            jax.ShapeDtypeStruct(tokens.shape, BF16),
            jax.ShapeDtypeStruct((toks, feats), BF16),
            jax.ShapeDtypeStruct((1, rows, feats), BF16),
        ),
        (last_block, whole((toks, feats)), whole((1, rows, feats))),
        4 * toks * rows * feats,
        2 * (2 * toks * rows + rows * feats) + 8 * toks * feats + 10 * rows * feats,
        {8: 0},
    )
    return (values, token_grad, weight_grad, new_momentum, new_global)


def solution(mesh):
    in_specs = (
        P(("rep", "fsdp"), None),
        P(("rep", "fsdp"), None),
        P("rep", "fsdp", None),
        P("rep", "fsdp", None),
        P("fsdp", None),
        P("fsdp", None),
    )
    out_specs = (
        P(("rep", "fsdp"), None),
        P(("rep", "fsdp"), None),
        P("rep", "fsdp", None),
        P("fsdp", None),
        P("fsdp", None),
    )
    return jax.shard_map(local, mesh=mesh, in_specs=in_specs, out_specs=out_specs, check_vma=False)
```
